32 devices in a mesh: groups: 2 (over x), expert: 16 (over z, y, core), cuts: 1.
Axes of the slice: x: 2, y: 2, z: 4, core: 2. Of those that a mesh axis runs over, the one named last changes fastest.
Arguments:
- quant: bfloat16 [512, 3584], P(('groups', 'expert', 'cuts')), parts along dimension 0, may hold values from -6 to 6
- scales: bfloat16 [512, 28], P(('groups', 'expert', 'cuts')), parts along dimension 0, may hold values from 0.29882812 to 3
- routes: int32 [512, 8], P(('groups', 'expert', 'cuts')), parts along dimension 0, may hold values from 0 to 15, all different within a row; in each aligned block of 16 rows (0 to 15, 16 to 31, ...) at most 12 rows name the same one
- gates: float32 [512, 8], P(('groups', 'expert', 'cuts')), parts along dimension 0, may hold values from 0.05 to 0.25
- cotangent: bfloat16 [512, 3584], P(('groups', 'expert', 'cuts')), parts along dimension 0, may hold values from -1.5 to 1.5
- w_gate: bfloat16 [16, 3584, 1280], P('expert', None, 'cuts'), may hold values from -0.09375 to 0.09375
- w_up: bfloat16 [16, 3584, 1280], P('expert', None, 'cuts'), may hold values from -0.09375 to 0.09375
- w_down: bfloat16 [16, 1280, 3584], P('expert', 'cuts'), may hold values from -0.15625 to 0.15625
Outputs:
- mixed: bfloat16 [512, 3584], P(('groups', 'expert', 'cuts')), parts along dimension 0
- grad_tokens: bfloat16 [512, 3584], P(('groups', 'expert', 'cuts')), parts along dimension 0
- grad_gates: float32 [512, 8], P(('groups', 'expert', 'cuts')), parts along dimension 0
- grad_up: bfloat16 [32, 3584, 1280], P(('groups', 'expert'), None, 'cuts'), parts along dimension 0
- grad_down: bfloat16 [32, 1280, 3584], P(('groups', 'expert'), 'cuts'), parts along dimension 0
The draws below stay inside these ranges and needn't reach their ends.
There are 2 independent parts, one for each index of `groups`. The reference program is written for one: setup_inputs(seed, part) draws one part's arguments, and reference() takes and returns one part's arrays. A program takes and returns all parts, laid end to end along the dimension named above; an argument that names none is the same for every part. Nothing has to cross between parts.
Inputs may be any that keep to these rules, and one draw needn't show every extreme that they name: `routes`: each row names 8 different experts. Within the 16 rows of one device no expert is named by more than 12 rows, and in some device's rows some expert is named by exactly 12.
All inputs are finite; a program needn't handle non-finite values.
Results may differ from the reference program's by a relative error of at most 0.0072.
Values may be sent and summed in bfloat16 or wider, within the bound.
A program may use at most 128 MiB of HBM per device.

```python
import math
import jax
import jax.numpy as jnp
import numpy as np
from jax import lax

D = 3584
FF = 1280
TOPK = 8
BLOCK = 128
TOK_DEV = 16
EXPERTS = 16
CAP = 12
TOKENS = 256
NBLK = 28


def block_levels(stream_key, extent, pieces, low, top_value):
    level = 1.0
    for position, shards_of in pieces:
        draws = jax.random.uniform(jax.random.fold_in(jax.random.fold_in(stream_key, 6), position), (shards_of,), jnp.float32, low / len(pieces), top_value / len(pieces))
        level = level * jnp.repeat(jnp.exp(draws), extent[position] // shards_of).reshape((-1,) + (1,) * (len(extent) - 1 - position))
    return level


def deal_out(key, own, number, rows, count, top, most, lean):
    ranking = jax.random.permutation(key, count)
    heavy_load, ordinary = shares(count, rows * top, most, lean, True), shares(count, rows * top, most, lean, False)
    places = jnp.arange(count)

    def named(lengths, offset_by):
        used = int((lengths > 0).sum())
        fixed = max(1, used // 4)
        moved = fixed + (places - fixed + offset_by * (used - fixed)) % max(1, count - fixed)
        return jnp.zeros((count,), jnp.int32).at[ranking[jnp.where(places < fixed, places, moved)]].set(jnp.asarray(lengths, jnp.int32))

    lengths = jnp.where(number % 4 == 0, named(heavy_load, number // 4), named(ordinary, number - number // 4 - 1))
    mixed = jax.random.permutation(jax.random.fold_in(own, 3), count)
    donor, sink = mixed[0:count // 2 * 2:2], mixed[1:count // 2 * 2:2]
    room = jnp.minimum(lengths[donor] - 1, most - lengths[sink]) // 2
    room = jnp.where((donor == ranking[0]) | (sink == ranking[0]) | (lengths[sink] == 0), 0, jnp.maximum(room, 0))
    moved = jax.random.randint(jax.random.fold_in(own, 4), (count // 2,), 0, 1 << 20) % (room + 1)
    lengths = lengths.at[donor].add(-moved).at[sink].add(moved)
    labels = jnp.searchsorted(jnp.cumsum(lengths), jnp.arange(rows * top), side="right").astype(jnp.int32)
    listing = labels.reshape(top, rows).T
    listing = listing[jax.random.permutation(jax.random.fold_in(own, 1), rows)]
    offset_by = jax.random.randint(jax.random.fold_in(own, 2), (rows, 1), 0, top)
    return jnp.take_along_axis(listing, (jnp.arange(top)[None, :] + offset_by) % top, axis=1)


def shares(count, total, bound, slope, full):
    portions = [(1 << 20) // math.isqrt(grade ** slope) + 1 for grade in range(1, count + 1)]
    largest = bound if full else min(bound, max(-(-total // count), total * portions[0] // sum(portions)))
    least = 1 if total - largest >= count - 1 else 0
    holding, rest = [largest] + [least] * (count - 1), total - largest - least * (count - 1)
    while rest > 0:
        movable = [i for i in range(1, count) if holding[i] < largest] or [i for i in range(1, count) if holding[i] < bound]
        mass, remaining = sum([portions[i] for i in movable]), rest
        for i in movable:
            extra = min(bound - holding[i], max(1, remaining * portions[i] // mass), rest)
            holding[i] = holding[i] + extra
            rest = rest - extra
    return np.array(holding)


def bell_draw(key, shape, scale, most, pieces=(), kind=jnp.bfloat16):
    loudness = block_levels(key, shape, pieces, -0.22, 0.18) if pieces else 1.0
    drawn = jax.random.normal(key, shape, jnp.float32) * scale * loudness
    return jnp.minimum(jnp.maximum(drawn, -most), most).astype(kind)


def setup_inputs(seed: int = 0, part: int = 0) -> dict:
    splits = jax.random.split(jax.random.key(seed), 9)
    part_splits = jax.random.split(jax.random.fold_in(splits[8], part), 9)
    quant = bell_draw(part_splits[0], (TOKENS, D), 1.0, 6.0, ((0, 16),))
    scales = jnp.clip(jnp.exp(math.log(3.0) - 2.306499 * jax.random.uniform(part_splits[1], (TOKENS, NBLK), jnp.float32) ** block_levels(part_splits[1], (TOKENS, NBLK), ((0, 16),), -0.2, 0.2)), 0.29882812, 3.0).astype(jnp.bfloat16)
    routes_keys = jax.random.split(jax.random.fold_in(part_splits[2], 1), TOKENS // TOK_DEV)
    routes_turns = jax.random.permutation(jax.random.fold_in(part_splits[2], 3), TOKENS // TOK_DEV)
    routes = jax.vmap(lambda own, number: deal_out(jax.random.fold_in(part_splits[2], 2), own, number, TOK_DEV, EXPERTS, TOPK, CAP, 2))(routes_keys, routes_turns).reshape((TOKENS, TOPK))
    gates = jnp.clip(0.05 + 0.2 * jax.random.uniform(part_splits[3], (TOKENS, TOPK), jnp.float32) ** block_levels(part_splits[3], (TOKENS, TOPK), ((0, 16),), -0.2, 0.2), 0.05, 0.25)
    cotangent = bell_draw(part_splits[4], (TOKENS, D), 0.25, 1.5, ((0, 16),))
    w_gate = bell_draw(splits[5], (EXPERTS, D, FF), D ** -0.5, 0.09375, ((0, 16),))
    w_up = bell_draw(splits[6], (EXPERTS, D, FF), D ** -0.5, 0.09375, ((0, 16),))
    w_down = bell_draw(splits[7], (EXPERTS, FF, D), FF ** -0.5, 0.15625, ((0, 16),))
    return dict(quant=quant, scales=scales, routes=routes, gates=gates, cotangent=cotangent, w_gate=w_gate, w_up=w_up, w_down=w_down)


def expert_pass(inputs, row_grad, weight_gate, weight_up, weight_down):
    gate_pre = jnp.dot(inputs, weight_gate, preferred_element_type=jnp.float32)
    up_pre = jnp.dot(inputs, weight_up, preferred_element_type=jnp.float32)
    gate_sig = jax.nn.sigmoid(gate_pre)
    activated = gate_pre * gate_sig
    hidden = (activated * up_pre).astype(jnp.bfloat16)
    output_part = jnp.dot(hidden, weight_down, preferred_element_type=jnp.float32)
    down_grad = lax.dot_general(hidden, row_grad, (((0,), (0,)), ((), ())), preferred_element_type=jnp.float32)
    hidden_grad = lax.dot_general(row_grad, weight_down, (((1,), (1,)), ((), ())), preferred_element_type=jnp.float32)
    gate_grad = (hidden_grad * up_pre * gate_sig * (1.0 + gate_pre * (1.0 - gate_sig))).astype(jnp.bfloat16)
    up_grad = (hidden_grad * activated).astype(jnp.bfloat16)
    up_weight_grad = lax.dot_general(inputs, up_grad, (((0,), (0,)), ((), ())), preferred_element_type=jnp.float32)
    input_part = lax.dot_general(gate_grad, weight_gate, (((1,), (1,)), ((), ())), preferred_element_type=jnp.float32)
    input_part = input_part + lax.dot_general(up_grad, weight_up, (((1,), (1,)), ((), ())), preferred_element_type=jnp.float32)
    return output_part, input_part, down_grad, up_weight_grad


def reference(quant, scales, routes, gates, cotangent, w_gate, w_up, w_down):
    count = quant.shape[0]
    inputs = (quant.astype(jnp.float32).reshape(count, NBLK, BLOCK) * scales.astype(jnp.float32)[:, :, None]).reshape(count, D).astype(jnp.bfloat16)
    scaled = (gates[:, :, None] * cotangent.astype(jnp.float32)[:, None, :]).astype(jnp.bfloat16)

    def per_expert(expert):
        picked = routes == expert
        row_grad = jnp.sum(jnp.where(picked[:, :, None], scaled.astype(jnp.float32), jnp.float32(0.0)), 1).astype(jnp.bfloat16)
        output_part, input_part, down_grad, up_weight_grad = expert_pass(inputs, row_grad, w_gate[expert], w_up[expert], w_down[expert])
        return (output_part.astype(jnp.bfloat16), input_part.astype(jnp.bfloat16), up_weight_grad.astype(jnp.bfloat16), down_grad.astype(jnp.bfloat16))

    expert_out, expert_dx, grad_up, grad_down = lax.map(per_expert, jnp.arange(EXPERTS, dtype=jnp.int32))
    token_index = jnp.arange(count, dtype=jnp.int32)[:, None]
    chosen_out = expert_out[routes, token_index].astype(jnp.float32)
    chosen_dx = expert_dx[routes, token_index].astype(jnp.float32)
    mixed = jnp.sum(gates[:, :, None] * chosen_out, 1).astype(jnp.bfloat16)
    grad_tokens = jnp.sum(chosen_dx, 1).astype(jnp.bfloat16)
    grad_gates = jnp.sum(cotangent.astype(jnp.float32)[:, None, :] * chosen_out, -1)
    return mixed, grad_tokens, grad_gates, grad_up, grad_down
```

```python
import jax
import jax.numpy as jnp
from jax import lax
from jax.sharding import PartitionSpec as P

AXES = ("expert", "cuts")


def local(quant, scales, routes, gates, cotangent, w_gate, w_up, w_down):
    cut_count = lax.axis_size("cuts")
    expert_count = lax.axis_size("expert")
    me = lax.axis_index("expert") * cut_count + lax.axis_index("cuts")
    count, width = quant.shape
    blocks = scales.shape[1]
    inputs = (
        (
            quant.astype(jnp.float32).reshape(count, blocks, width // blocks)
            * scales.astype(jnp.float32)[:, :, None]
        )
        .reshape(count, width)
        .astype(jnp.bfloat16)
    )
    expert_ids = lax.broadcasted_iota(jnp.int32, (1, 1, expert_count), 2)
    onehot = (routes[:, :, None] == expert_ids).astype(jnp.float32)
    weight_of = jnp.sum(gates[:, :, None] * onehot, 1)
    x_all = lax.all_gather(inputs, AXES, axis=0, tiled=True)
    weight_all = lax.all_gather(weight_of, AXES, axis=0, tiled=True)
    cot_all = lax.all_gather(cotangent, AXES, axis=0, tiled=True)
    mine = lax.broadcasted_iota(jnp.int32, (1, expert_count), 1) == lax.axis_index("expert")
    weight = jnp.sum(jnp.where(mine, weight_all, 0.0), 1, keepdims=True)
    cot_float = cot_all.astype(jnp.float32)
    row_grad = (weight * cot_float).astype(jnp.bfloat16)

    wg, wu, wd = w_gate[0], w_up[0], w_down[0]
    gate_pre = jnp.dot(x_all, wg, preferred_element_type=jnp.float32)
    up_pre = jnp.dot(x_all, wu, preferred_element_type=jnp.float32)
    sig = jax.nn.sigmoid(gate_pre)
    act = gate_pre * sig
    hidden = (act * up_pre).astype(jnp.bfloat16)
    out = jnp.dot(hidden, wd, preferred_element_type=jnp.float32)
    dots = jnp.sum(cot_float * out, 1, keepdims=True)
    mixed = lax.psum_scatter(
        (weight * out).astype(jnp.bfloat16), AXES, scatter_dimension=0, tiled=True
    )
    dots_home = lax.psum_scatter(
        jnp.where(mine, dots, 0.0), AXES, scatter_dimension=0, tiled=True
    )
    nt = (((1,), (1,)), ((), ()))
    tn = (((0,), (0,)), ((), ()))
    hidden_grad = lax.dot_general(row_grad, wd, nt, preferred_element_type=jnp.float32)
    gate_grad = (hidden_grad * up_pre * sig * (1.0 + gate_pre * (1.0 - sig))).astype(jnp.bfloat16)
    up_grad = (hidden_grad * act).astype(jnp.bfloat16)
    dx = lax.dot_general(gate_grad, wg, nt, preferred_element_type=jnp.float32)
    dx = dx + lax.dot_general(up_grad, wu, nt, preferred_element_type=jnp.float32)
    grad_tokens = lax.psum_scatter(
        dx.astype(jnp.bfloat16), AXES, scatter_dimension=0, tiled=True
    )
    grad_up = lax.dot_general(x_all, up_grad, tn, preferred_element_type=jnp.float32)
    grad_down = lax.dot_general(hidden, row_grad, tn, preferred_element_type=jnp.float32)
    grad_gates = jnp.sum(onehot * dots_home[:, None, :], -1)
    return (
        mixed,
        grad_tokens,
        grad_gates,
        grad_up.astype(jnp.bfloat16)[None],
        grad_down.astype(jnp.bfloat16)[None],
    )


def solution(mesh):
    rows = P(("groups", "expert", "cuts"), None)
    in_specs = (rows,) * 5 + (P("expert", None, "cuts"), P("expert", None, "cuts"), P("expert", "cuts", None))
    out_specs = (rows,) * 3 + (
        P(("groups", "expert"), None, "cuts"),
        P(("groups", "expert"), "cuts", None),
    )
    return jax.shard_map(local, mesh=mesh, in_specs=in_specs, out_specs=out_specs, check_vma=False)
```

```python
import functools

import jax
import jax.numpy as jnp
from jax import lax
from jax.experimental import pallas as pl
from jax.experimental.pallas import tpu as pltpu
from jax.sharding import PartitionSpec as P

MESH = pl.DeviceIdType.MESH
LANES = 128
NT = (((1,), (1,)), ((), ()))
TN = (((0,), (0,)), ((), ()))
F32 = jnp.float32
BF16 = jnp.bfloat16


def parts_of(value):
    high = value.astype(BF16)
    rest = value - high.astype(F32)
    middle = rest.astype(BF16)
    return high, middle, (rest - middle.astype(F32)).astype(BF16)


def kernel(
    experts, cuts, quant, scales, routes, gates, cot, wg_hbm, wu_hbm, wd_hbm,
    mixed, grad_tokens, grad_gates, x_out, up_out, hidden_out, row_out,
    xg, cg, wg, wu, wd, rg, hidden, gate_grad, up_grad, slope, act, weight, dot_acc,
    mix_part, dx_part, sib_mix, sib_dx, out_r, in_r, out_l, in_l,
    w_sem, o_sem, gs_sem, gr_sem, rs_sem, rr_sem,
):
    devices = experts * cuts
    ring = devices // 2
    hops_r = ring // 2
    hops_l = ring - 1 - hops_r
    count, width = quant.shape
    rows = devices * count
    hid = wg.shape[1]
    tile = 256 if hid % 256 == 0 else 128
    col = 256
    half = width // 2

    expert = lax.axis_index("expert")
    me = expert * cuts + lax.axis_index("cuts")
    core = lax.rem(me, 2)
    chip = me // 2

    def chip_at(p):
        if cuts > 1:
            return p
        upper = p // hops_r
        return upper * (2 * (ring - 1 - p) + 1) + (1 - upper) * 2 * p

    if cuts > 1:
        pos = chip
    else:
        y = lax.rem(chip, 2)
        z = chip // 2
        pos = z + y * (ring - 1 - 2 * z)

    def wrap(p):
        return lax.rem(p + 2 * ring, ring)

    def device(p, c):
        i = chip_at(p) * 2 + c
        return {"expert": i // cuts, "cuts": lax.rem(i, cuts)}

    right = device(wrap(pos + 1), core)
    left = device(wrap(pos - 1), core)
    sibling = device(pos, 1 - core)

    loads = [
        pltpu.make_async_copy(src.at[0], dst, w_sem.at[n])
        for n, (src, dst) in enumerate(((wg_hbm, wg), (wu_hbm, wu), (wd_hbm, wd)))
    ]
    for load in loads:
        load.start()

    own = core * ring + pos
    for b in range(scales.shape[1]):
        block = pl.ds(b * (width // scales.shape[1]), width // scales.shape[1])
        xg[own, :, block] = (
            quant[:, block].astype(F32) * scales[:, b : b + 1].astype(F32)
        ).astype(BF16)
    lane = lax.broadcasted_iota(jnp.int32, (count, LANES), 1)
    pay = jnp.zeros((count, LANES), F32)
    for k in range(routes.shape[1]):
        pay += jnp.where(lane == routes[:, k : k + 1], gates[:, k : k + 1], 0.0)
    cg[own, :, 0:width] = cot[...]
    packed = jnp.zeros((count, LANES), F32)
    for n, part in enumerate(parts_of(pay)):
        part = part.astype(F32)
        shifted = part if n == 0 else pltpu.roll(part, n * experts, 1)
        packed += shifted
    cg[own, :, width : width + LANES] = packed.astype(BF16)

    barrier = pltpu.get_barrier_semaphore()
    for other in (left, right, sibling):
        pl.semaphore_signal(barrier, inc=1, device_id=other, device_id_type=MESH)
    pl.semaphore_wait(barrier, 3)

    sends = []

    def gather(which, buf):
        def move(p, c, n, to):
            ref = buf.at[c * ring + p]
            return pltpu.make_async_remote_copy(
                src_ref=ref, dst_ref=ref, send_sem=gs_sem.at[which, n],
                recv_sem=gr_sem.at[which, n], device_id=to, device_id_type=MESH,
            )

        def go(p, n, to):
            copy = move(p, core, n, to)
            copy.start()
            sends.append(copy)

        def step(s):
            if s == 0:
                go(pos, 0, right)
                go(pos, hops_r, left)
                go(pos, ring, sibling)
                return
            if s - 1 < hops_r:
                p = wrap(pos - s)
                move(p, core, s - 1, right).wait_recv()
                if s < hops_r:
                    go(p, s, right)
                go(p, ring + s, sibling)
            if s - 1 < hops_l:
                p = wrap(pos + s)
                move(p, core, hops_r + s - 1, left).wait_recv()
                if s < hops_l:
                    go(p, hops_r + s, left)
                go(p, ring + hops_r + s, sibling)

        def finish():
            for k in range(ring):
                p = pos - k if k <= hops_r else pos + (k - hops_r)
                move(wrap(p), 1 - core, ring + k, sibling).wait_recv()

        return step, finish

    x_step, x_finish = gather(0, xg)
    c_step, c_finish = gather(1, cg)
    lag = 2
    for s in range(hops_r + 1):
        x_step(s)
        if s >= lag:
            c_step(s - lag)
    x_finish()
    outs = []

    def store(n, src, dst):
        copy = pltpu.make_async_copy(src, dst, o_sem.at[n])
        copy.start()
        outs.append(copy)

    store(0, xg, x_out)

    def up_tiles(first, last):
        @pl.loop(first, last)
        def _(n):
            cols = pl.ds(pl.multiple_of(n * tile, tile), tile)
            x = xg[...].reshape(rows, width)
            gate = jnp.dot(x, wg[:, cols], preferred_element_type=F32)
            up = jnp.dot(x, wu[:, cols], preferred_element_type=F32)
            sig = jax.nn.sigmoid(gate)
            active = gate * sig
            act[:, cols] = active
            slope[:, cols] = up * sig * (1.0 + gate * (1.0 - sig))
            hidden[:, cols] = (active * up).astype(BF16)

    loads[0].wait()
    loads[1].wait()
    tiles = hid // tile
    up_tiles(0, 1)
    c_step(hops_r - 1)
    up_tiles(1, 3)
    c_step(hops_r)
    up_tiles(3, tiles)
    c_finish()
    store(1, hidden, hidden_out)

    row_lane = lax.broadcasted_iota(jnp.int32, (rows, LANES), 1)
    mine = (row_lane == expert) | (row_lane == expert + experts)
    mine = mine | (row_lane == expert + 2 * experts)
    got = cg[:, :, width : width + LANES].reshape(rows, LANES).astype(F32)
    weight[...] = jnp.broadcast_to(
        jnp.sum(jnp.where(mine, got, 0.0), 1, keepdims=True), (rows, LANES)
    )
    loads[2].wait()
    dot_acc[...] = jnp.zeros_like(dot_acc)

    def out_tiles(first, last):
        @pl.loop(first, last)
        def _(n):
            cols = pl.ds(pl.multiple_of(n * col, col), col)
            out = jnp.dot(hidden[...], wd[:, cols], preferred_element_type=F32)
            c = cg[:, :, cols].reshape(rows, col).astype(F32)
            w = weight[:, 0:1]
            dot_acc[...] += c * out
            rg[:, cols] = (w * c).astype(BF16)
            mix_part[:, :, cols] = (w * out).astype(BF16).reshape(devices, count, col)

    def reduce(job, buf, sib, lo, wide):
        cols = pl.ds(lo, wide)
        narrow = pl.ds(0, wide)

        def copy(src, dst, n, to):
            return pltpu.make_async_remote_copy(
                src_ref=src, dst_ref=dst, send_sem=rs_sem.at[job, n],
                recv_sem=rr_sem.at[job, n], device_id=to, device_id_type=MESH,
            )

        def swap_cores():
            c = copy(
                buf.at[pl.ds((1 - core) * ring, ring), :, cols], sib, ring, sibling
            )
            c.start()
            sends.append(c)
            return c

        state = {}

        def begin():
            state["sib"] = swap_cores()

        def base(p):
            return buf[core * ring + p, :, cols].astype(F32) + sib[p].astype(F32)

        def ring_copy(s, go_right):
            if go_right:
                return copy(out_r.at[job, s, :, narrow], in_r.at[job, s, :, narrow], s, right)
            return copy(out_l.at[job, s, :, narrow], in_l.at[job, s, :, narrow], hops_r + s, left)

        def hop(s):
            if s == 0:
                state["sib"].wait_recv()
            for go_right, hops, outb, inb in (
                (True, hops_r, out_r, in_r), (False, hops_l, out_l, in_l)
            ):
                if s >= hops:
                    continue
                p = wrap(pos + hops - s) if go_right else wrap(pos - hops + s)
                total = base(p)
                if s > 0:
                    ring_copy(s - 1, go_right).wait_recv()
                    total += inb[job, s - 1, :, narrow].astype(F32)
                outb[job, s, :, narrow] = total.astype(BF16)
                c = ring_copy(s, go_right)
                c.start()
                sends.append(c)

        def last():
            ring_copy(hops_r - 1, True).wait_recv()
            ring_copy(hops_l - 1, False).wait_recv()
            return (
                base(pos)
                + in_r[job, hops_r - 1, :, narrow].astype(F32)
                + in_l[job, hops_l - 1, :, narrow].astype(F32)
            )

        return begin, hop, last

    mix0 = reduce(0, mix_part, sib_mix.at[0, :, :, pl.ds(0, half)], 0, half)
    mix1 = reduce(1, mix_part, sib_mix.at[1], half, half + LANES)
    dx0 = reduce(2, dx_part, sib_dx.at[0], 0, half)
    dx1 = reduce(3, dx_part, sib_dx.at[1], half, half)

    per_half = half // col
    out_tiles(0, per_half)
    mix0[0]()
    out_tiles(per_half, 2 * per_half)
    store(2, rg, row_out)
    dots = jnp.sum(dot_acc[...], 1, keepdims=True)
    extra = jnp.zeros((rows, LANES), F32)
    for n, part in enumerate(parts_of(dots)):
        extra += jnp.where(row_lane == me + n * devices, part.astype(F32), 0.0)
    mix_part[:, :, width : width + LANES] = extra.astype(BF16).reshape(devices, count, LANES)
    mix1[0]()
    mix0[1](0)

    @pl.loop(0, tiles)
    def _(n):
        cols = pl.ds(pl.multiple_of(n * tile, tile), tile)
        grad = lax.dot_general(rg[...], wd[cols, :], NT, preferred_element_type=F32)
        gate_grad[:, cols] = (grad * slope[:, cols]).astype(BF16)
        up_grad[:, cols] = (grad * act[:, cols]).astype(BF16)

    store(3, up_grad, up_out)
    mix1[1](0)
    mix0[1](1)

    def dx_tiles(first, last):
        @pl.loop(first, last)
        def _(n):
            cols = pl.ds(pl.multiple_of(n * col, col), col)
            dx = lax.dot_general(gate_grad[...], wg[cols, :], NT, preferred_element_type=F32)
            dx += lax.dot_general(up_grad[...], wu[cols, :], NT, preferred_element_type=F32)
            dx_part[:, :, cols] = dx.astype(BF16).reshape(devices, count, col)

    mid = per_half // 2
    dx_tiles(0, mid)
    mix1[1](1)
    mix0[1](2)
    dx_tiles(mid, per_half)
    dx0[0]()
    mix1[1](2)
    mix0[1](3)
    dx_tiles(per_half, per_half + mid)
    dx0[1](0)
    mix1[1](3)
    dx_tiles(per_half + mid, 2 * per_half)
    dx1[0]()
    for s in range(4, hops_r):
        mix0[1](s)
        mix1[1](s)
    for s in range(1, hops_r):
        dx0[1](s)
        dx1[1](s - 1)
    dx1[1](hops_r - 1)

    mixed[:, 0:half] = mix0[2]().astype(BF16)
    rest = mix1[2]()
    mixed[:, half:width] = rest[:, 0:half].astype(BF16)
    sums = rest[:, half : half + LANES]
    slot = lax.broadcasted_iota(jnp.int32, (count, routes.shape[1]), 1)
    found = jnp.zeros((count, routes.shape[1]), F32)
    for k in range(routes.shape[1]):
        base_lane = routes[:, k : k + 1] * cuts
        picked = lane < 0
        for n in range(3):
            for c in range(cuts):
                picked = picked | (lane == base_lane + (c + n * devices))
        value = jnp.sum(jnp.where(picked, sums, 0.0), 1, keepdims=True)
        found += jnp.where(slot == k, value, 0.0)
    grad_gates[...] = found
    grad_tokens[:, 0:half] = dx0[2]().astype(BF16)
    grad_tokens[:, half:width] = dx1[2]().astype(BF16)

    for copy in sends:
        copy.wait_send()
    for copy in outs:
        copy.wait()


def local(quant, scales, routes, gates, cotangent, w_gate, w_up, w_down):
    cuts = lax.axis_size("cuts")
    experts = lax.axis_size("expert")
    devices = experts * cuts
    ring = devices // 2
    hops_r = ring // 2
    hops_l = ring - 1 - hops_r
    count, width = quant.shape
    hid = w_gate.shape[2]
    rows = devices * count
    half = width // 2
    vmem = pl.BlockSpec(memory_space=pltpu.VMEM)
    hbm = pl.BlockSpec(memory_space=pl.ANY)
    sds = jax.ShapeDtypeStruct
    dma = pltpu.SemaphoreType.DMA
    mixed, grad_tokens, grad_gates, x_all, up_grad, hidden, row_grad = pl.pallas_call(
        functools.partial(kernel, experts, cuts),
        out_shape=(
            sds((count, width), BF16),
            sds((count, width), BF16),
            sds(gates.shape, F32),
            sds((devices, count, width), BF16),
            sds((rows, hid), BF16),
            sds((rows, hid), BF16),
            sds((rows, width), BF16),
        ),
        in_specs=[vmem] * 5 + [hbm] * 3,
        out_specs=(vmem,) * 3 + (hbm,) * 4,
        scratch_shapes=[
            pltpu.VMEM((devices, count, width), BF16),
            pltpu.VMEM((devices, count, width + LANES), BF16),
            pltpu.VMEM((width, hid), BF16),
            pltpu.VMEM((width, hid), BF16),
            pltpu.VMEM((hid, width), BF16),
            pltpu.VMEM((rows, width), BF16),
            pltpu.VMEM((rows, hid), BF16),
            pltpu.VMEM((rows, hid), BF16),
            pltpu.VMEM((rows, hid), BF16),
            pltpu.VMEM((rows, hid), F32),
            pltpu.VMEM((rows, hid), F32),
            pltpu.VMEM((rows, LANES), F32),
            pltpu.VMEM((rows, 256), F32),
            pltpu.VMEM((devices, count, width + LANES), BF16),
            pltpu.VMEM((devices, count, width), BF16),
            pltpu.VMEM((2, ring, count, half + LANES), BF16),
            pltpu.VMEM((2, ring, count, half), BF16),
            pltpu.VMEM((4, hops_r, count, half + LANES), BF16),
            pltpu.VMEM((4, hops_r, count, half + LANES), BF16),
            pltpu.VMEM((4, hops_l, count, half + LANES), BF16),
            pltpu.VMEM((4, hops_l, count, half + LANES), BF16),
            dma((3,)),
            dma((4,)),
            dma((2, 2 * ring)),
            dma((2, 2 * ring)),
            dma((4, ring + 1)),
            dma((4, ring + 1)),
        ],
        compiler_params=pltpu.CompilerParams(
            collective_id=0, has_side_effects=True, vmem_limit_bytes=60 * 1024 * 1024
        ),
        cost_estimate=pl.CostEstimate(
            flops=12 * rows * width * hid,
            bytes_accessed=6 * width * hid + 4 * rows * (width + hid),
            transcendentals=rows * hid,
        ),
    )(quant, scales, routes, gates, cotangent, w_gate, w_up, w_down)
    x_all = x_all.reshape(rows, width)
    grad_up = lax.dot_general(x_all, up_grad, TN, preferred_element_type=F32)
    grad_down = lax.dot_general(hidden, row_grad, TN, preferred_element_type=F32)
    return (
        mixed,
        grad_tokens,
        grad_gates,
        grad_up.astype(BF16)[None],
        grad_down.astype(BF16)[None],
    )


def solution(mesh):
    rows = P(("groups", "expert", "cuts"), None)
    in_specs = (rows,) * 5 + (
        P("expert", None, "cuts"),
        P("expert", None, "cuts"),
        P("expert", "cuts", None),
    )
    out_specs = (rows,) * 3 + (
        P(("groups", "expert"), None, "cuts"),
        P(("groups", "expert"), "cuts", None),
    )
    return jax.shard_map(local, mesh=mesh, in_specs=in_specs, out_specs=out_specs, check_vma=False)
```

```python
import functools

import jax
import jax.numpy as jnp
from jax import lax
from jax.experimental import pallas as pl
from jax.experimental.pallas import tpu as pltpu
from jax.sharding import PartitionSpec as P

MESH = pl.DeviceIdType.MESH
LANES = 128
NT = (((1,), (1,)), ((), ()))
TN = (((0,), (0,)), ((), ()))
F32 = jnp.float32
BF16 = jnp.bfloat16


def parts_of(value):
    high = value.astype(BF16)
    rest = value - high.astype(F32)
    middle = rest.astype(BF16)
    return high, middle, (rest - middle.astype(F32)).astype(BF16)


def kernel(
    experts, cuts, quant, scales, routes, gates, cot, wg_hbm, wu_hbm, wd_hbm,
    mixed, grad_tokens, grad_gates, x_out, up_out, hidden_out, row_out,
    xg, cg, wg, wu, wd, rg, hidden, gate_grad, up_grad, slope, act, weight, dot_acc,
    mix_part, dx_part, sib_mix, sib_dx, out_r, in_r, out_l, in_l,
    turn, w_sem, o_sem, gs_sem, gr_sem, rs_sem, rr_sem,
):
    devices = experts * cuts
    ring = devices // 2
    count, width = quant.shape
    rows = devices * count
    hid = wg.shape[1]
    tile = 256 if hid % 256 == 0 else 128
    col = 256
    half = width // 2

    expert = lax.axis_index("expert")
    me = expert * cuts + lax.axis_index("cuts")
    core = lax.rem(me, 2)
    chip = me // 2

    def chip_at(p):
        if cuts > 1:
            return p
        upper = p // (ring // 2)
        return upper * (2 * (ring - 1 - p) + 1) + (1 - upper) * 2 * p

    if cuts > 1:
        pos = chip
    else:
        y = lax.rem(chip, 2)
        z = chip // 2
        pos = z + y * (ring - 1 - 2 * z)

    def wrap(p):
        return lax.rem(p + 2 * ring, ring)

    def device(p, c):
        i = chip_at(p) * 2 + c
        return {"expert": i // cuts, "cuts": lax.rem(i, cuts)}

    right = device(wrap(pos + 1), core)
    left = device(wrap(pos - 1), core)
    sibling = device(pos, 1 - core)

    loads = [
        pltpu.make_async_copy(src.at[0], dst, w_sem.at[n])
        for n, (src, dst) in enumerate(((wg_hbm, wg), (wu_hbm, wu), (wd_hbm, wd)))
    ]
    for load in loads:
        load.start()

    own = core * ring + pos
    for b in range(scales.shape[1]):
        block = pl.ds(b * (width // scales.shape[1]), width // scales.shape[1])
        xg[own, :, block] = (
            quant[:, block].astype(F32) * scales[:, b : b + 1].astype(F32)
        ).astype(BF16)
    tops = routes.shape[0]
    lane = lax.broadcasted_iota(jnp.int32, (count, LANES), 1)
    sub = lax.broadcasted_iota(jnp.int32, (LANES, count), 0)
    pay_t = jnp.zeros((LANES, count), F32)
    for k in range(tops):
        pay_t += jnp.where(sub == routes[k : k + 1, :], gates[k : k + 1, :], 0.0)
    turn[...] = jnp.zeros_like(turn)
    turn[:, 0:count] = pay_t
    pay = turn[...].T[0:count, :]
    cg[own, :, 0:width] = cot[...]
    packed = jnp.zeros((count, LANES), F32)
    for n, part in enumerate(parts_of(pay)):
        part = part.astype(F32)
        shifted = part if n == 0 else pltpu.roll(part, n * experts, 1)
        packed += shifted
    cg[own, :, width : width + LANES] = packed.astype(BF16)

    barrier = pltpu.get_barrier_semaphore()
    for other in (left, right, sibling):
        pl.semaphore_signal(barrier, inc=1, device_id=other, device_id_type=MESH)
    pl.semaphore_wait(barrier, 3)

    sends = []
    hops = ring // 2
    shares = ((hops, ring - 1 - hops), (ring - 1 - hops, hops))

    def gather(job, buf, lo, wide, hops_r, hops_l):
        def move(p, c, n, to):
            ref = buf.at[c * ring + p, :, pl.ds(lo, wide)]
            return pltpu.make_async_remote_copy(
                src_ref=ref, dst_ref=ref, send_sem=gs_sem.at[job, n],
                recv_sem=gr_sem.at[job, n], device_id=to, device_id_type=MESH,
            )

        def go(p, n, to):
            copy = move(p, core, n, to)
            copy.start()
            sends.append(copy)

        def step(s):
            if s == 0:
                go(pos, 0, right)
                go(pos, hops, left)
                go(pos, 2 * hops, sibling)
                return
            if s <= hops_r:
                p = wrap(pos - s)
                move(p, core, s - 1, right).wait_recv()
                if s < hops_r:
                    go(p, s, right)
                go(p, 2 * hops + s, sibling)
            if s <= hops_l:
                p = wrap(pos + s)
                move(p, core, hops + s - 1, left).wait_recv()
                if s < hops_l:
                    go(p, hops + s, left)
                go(p, 3 * hops + s, sibling)

        def finish():
            move(pos, 1 - core, 2 * hops, sibling).wait_recv()
            for s in range(1, hops_r + 1):
                move(wrap(pos - s), 1 - core, 2 * hops + s, sibling).wait_recv()
            for s in range(1, hops_l + 1):
                move(wrap(pos + s), 1 - core, 3 * hops + s, sibling).wait_recv()

        return step, finish

    x_jobs = [gather(0, xg, 0, half, *shares[0]), gather(1, xg, half, half, *shares[1])]
    c_jobs = [
        gather(2, cg, 0, half, *shares[0]),
        gather(3, cg, half, half + LANES, *shares[1]),
    ]
    for s in range(hops + 1):
        for step, _ in x_jobs:
            step(s)
        if s >= 1:
            for step, _ in c_jobs:
                step(s - 1)
    for _, finish in x_jobs:
        finish()
    outs = []

    def store(n, src, dst):
        copy = pltpu.make_async_copy(src, dst, o_sem.at[n])
        copy.start()
        outs.append(copy)

    store(0, xg, x_out)

    def up_tiles(first, last):
        @pl.loop(first, last)
        def _(n):
            cols = pl.ds(pl.multiple_of(n * tile, tile), tile)
            x = xg[...].reshape(rows, width)
            gate = jnp.dot(x, wg[:, cols], preferred_element_type=F32)
            up = jnp.dot(x, wu[:, cols], preferred_element_type=F32)
            sig = jax.nn.sigmoid(gate)
            active = gate * sig
            act[:, cols] = active
            slope[:, cols] = up * sig * (1.0 + gate * (1.0 - sig))
            hidden[:, cols] = (active * up).astype(BF16)

    loads[0].wait()
    loads[1].wait()
    tiles = hid // tile
    up_tiles(0, 1)
    for step, _ in c_jobs:
        step(hops)
    up_tiles(1, tiles)
    for _, finish in c_jobs:
        finish()
    store(1, hidden, hidden_out)

    row_lane = lax.broadcasted_iota(jnp.int32, (rows, LANES), 1)
    mine = (row_lane == expert) | (row_lane == expert + experts)
    mine = mine | (row_lane == expert + 2 * experts)
    got = cg[:, :, width : width + LANES].reshape(rows, LANES).astype(F32)
    weight[...] = jnp.broadcast_to(
        jnp.sum(jnp.where(mine, got, 0.0), 1, keepdims=True), (rows, LANES)
    )
    loads[2].wait()
    dot_acc[...] = jnp.zeros_like(dot_acc)

    def out_tiles(first, last):
        @pl.loop(first, last)
        def _(n):
            cols = pl.ds(pl.multiple_of(n * col, col), col)
            out = jnp.dot(hidden[...], wd[:, cols], preferred_element_type=F32)
            c = cg[:, :, cols].reshape(rows, col).astype(F32)
            w = weight[:, 0:1]
            dot_acc[...] += c * out
            rg[:, cols] = (w * c).astype(BF16)
            mix_part[:, :, cols] = (w * out).astype(BF16).reshape(devices, count, col)

    def reduce(job, buf, sib, lo, wide, hops_r, hops_l):
        cols = pl.ds(lo, wide)
        narrow = pl.ds(0, wide)

        def copy(src, dst, n, to):
            return pltpu.make_async_remote_copy(
                src_ref=src, dst_ref=dst, send_sem=rs_sem.at[job, n],
                recv_sem=rr_sem.at[job, n], device_id=to, device_id_type=MESH,
            )

        def swap_cores():
            c = copy(
                buf.at[pl.ds((1 - core) * ring, ring), :, cols], sib, 2 * hops, sibling
            )
            c.start()
            sends.append(c)
            return c

        state = {"next": 0}

        def begin():
            state["sib"] = swap_cores()

        def base(p):
            return buf[core * ring + p, :, cols].astype(F32) + sib[p].astype(F32)

        def ring_copy(s, go_right):
            if go_right:
                return copy(out_r.at[job, s, :, narrow], in_r.at[job, s, :, narrow], s, right)
            return copy(out_l.at[job, s, :, narrow], in_l.at[job, s, :, narrow], hops + s, left)

        def hop():
            s = state["next"]
            if s == hops:
                return
            state["next"] = s + 1
            if s == 0:
                state["sib"].wait_recv()
            for go_right, most, outb, inb in (
                (True, hops_r, out_r, in_r), (False, hops_l, out_l, in_l)
            ):
                if s >= most:
                    continue
                p = wrap(pos + most - s) if go_right else wrap(pos - most + s)
                total = base(p)
                if s > 0:
                    ring_copy(s - 1, go_right).wait_recv()
                    total += inb[job, s - 1, :, narrow].astype(F32)
                outb[job, s, :, narrow] = total.astype(BF16)
                c = ring_copy(s, go_right)
                c.start()
                sends.append(c)

        def last():
            ring_copy(hops_r - 1, True).wait_recv()
            ring_copy(hops_l - 1, False).wait_recv()
            return (
                base(pos)
                + in_r[job, hops_r - 1, :, narrow].astype(F32)
                + in_l[job, hops_l - 1, :, narrow].astype(F32)
            )

        return begin, hop, last

    mix0 = reduce(0, mix_part, sib_mix.at[0, :, :, pl.ds(0, half)], 0, half, *shares[0])
    mix1 = reduce(1, mix_part, sib_mix.at[1], half, half + LANES, *shares[1])
    dx0 = reduce(2, dx_part, sib_dx.at[0], 0, half, *shares[0])
    dx1 = reduce(3, dx_part, sib_dx.at[1], half, half, *shares[1])

    per_half = half // col
    out_tiles(0, per_half)
    mix0[0]()
    out_tiles(per_half, 2 * per_half)
    store(2, rg, row_out)
    dots = jnp.sum(dot_acc[...], 1, keepdims=True)
    extra = jnp.zeros((rows, LANES), F32)
    for n, part in enumerate(parts_of(dots)):
        extra += jnp.where(row_lane == me + n * devices, part.astype(F32), 0.0)
    mix_part[:, :, width : width + LANES] = extra.astype(BF16).reshape(devices, count, LANES)
    mix1[0]()
    mix0[1]()

    def hidden_tiles(first, last):
        @pl.loop(first, last)
        def _(n):
            cols = pl.ds(pl.multiple_of(n * tile, tile), tile)
            grad = lax.dot_general(rg[...], wd[cols, :], NT, preferred_element_type=F32)
            gate_grad[:, cols] = (grad * slope[:, cols]).astype(BF16)
            up_grad[:, cols] = (grad * act[:, cols]).astype(BF16)

    def dx_tiles(first, last):
        @pl.loop(first, last)
        def _(n):
            cols = pl.ds(pl.multiple_of(n * col, col), col)
            dx = lax.dot_general(gate_grad[...], wg[cols, :], NT, preferred_element_type=F32)
            dx += lax.dot_general(up_grad[...], wu[cols, :], NT, preferred_element_type=F32)
            dx_part[:, :, cols] = dx.astype(BF16).reshape(devices, count, col)

    hidden_tiles(0, 2)
    mix1[1]()
    mix0[1]()
    hidden_tiles(2, 4)
    mix1[1]()
    mix0[1]()
    hidden_tiles(4, tiles)
    store(3, up_grad, up_out)
    dx_tiles(0, 2)
    mix1[1]()
    mix0[1]()
    dx_tiles(2, 5)
    mix1[1]()
    dx_tiles(5, per_half)
    dx0[0]()
    dx_tiles(per_half, per_half + 2)
    dx0[1]()
    dx_tiles(per_half + 2, per_half + 5)
    dx0[1]()
    dx_tiles(per_half + 5, 2 * per_half)
    dx1[0]()
    dx0[1]()
    for _ in range(hops):
        for job in (mix0, mix1, dx1, dx0):
            job[1]()

    mixed[:, 0:half] = mix0[2]().astype(BF16)
    rest = mix1[2]()
    mixed[:, half:width] = rest[:, 0:half].astype(BF16)
    sums = rest[:, half : half + LANES]
    turn[0:count, :] = sums
    sums_t = turn[...].T[:, 0:count]
    for k in range(tops):
        base_lane = routes[k : k + 1, :] * cuts
        picked = sub < 0
        for n in range(3):
            for c in range(cuts):
                picked = picked | (sub == base_lane + (c + n * devices))
        grad_gates[k : k + 1, :] = jnp.sum(jnp.where(picked, sums_t, 0.0), 0, keepdims=True)
    grad_tokens[:, 0:half] = dx0[2]().astype(BF16)
    grad_tokens[:, half:width] = dx1[2]().astype(BF16)

    for copy in sends:
        copy.wait_send()
    for copy in outs:
        copy.wait()


def weight_grads(x, up_grad, hidden, row_grad, grad_up, grad_down, hidden_t):
    @pl.when(pl.program_id(0) == 0)
    def _():
        hidden_t[...] = hidden[...].T

    grad_up[0] = lax.dot_general(
        x[...], up_grad[...], TN, preferred_element_type=F32
    ).astype(BF16)
    grad_down[0] = jnp.dot(
        hidden_t[...], row_grad[...], preferred_element_type=F32
    ).astype(BF16)


def local(quant, scales, routes, gates, cotangent, w_gate, w_up, w_down):
    cuts = lax.axis_size("cuts")
    experts = lax.axis_size("expert")
    devices = experts * cuts
    ring = devices // 2
    hops = ring // 2
    count, width = quant.shape
    hid = w_gate.shape[2]
    rows = devices * count
    half = width // 2
    vmem = pl.BlockSpec(memory_space=pltpu.VMEM)
    hbm = pl.BlockSpec(memory_space=pl.ANY)
    sds = jax.ShapeDtypeStruct
    dma = pltpu.SemaphoreType.DMA
    mixed, grad_tokens, grad_gates, x_all, up_grad, hidden, row_grad = pl.pallas_call(
        functools.partial(kernel, experts, cuts),
        out_shape=(
            sds((count, width), BF16),
            sds((count, width), BF16),
            sds(gates.shape[::-1], F32),
            sds((devices, count, width), BF16),
            sds((rows, hid), BF16),
            sds((rows, hid), BF16),
            sds((rows, width), BF16),
        ),
        in_specs=[vmem] * 5 + [hbm] * 3,
        out_specs=(vmem,) * 3 + (hbm,) * 4,
        scratch_shapes=[
            pltpu.VMEM((devices, count, width), BF16),
            pltpu.VMEM((devices, count, width + LANES), BF16),
            pltpu.VMEM((width, hid), BF16),
            pltpu.VMEM((width, hid), BF16),
            pltpu.VMEM((hid, width), BF16),
            pltpu.VMEM((rows, width), BF16),
            pltpu.VMEM((rows, hid), BF16),
            pltpu.VMEM((rows, hid), BF16),
            pltpu.VMEM((rows, hid), BF16),
            pltpu.VMEM((rows, hid), F32),
            pltpu.VMEM((rows, hid), F32),
            pltpu.VMEM((rows, LANES), F32),
            pltpu.VMEM((rows, 256), F32),
            pltpu.VMEM((devices, count, width + LANES), BF16),
            pltpu.VMEM((devices, count, width), BF16),
            pltpu.VMEM((2, ring, count, half + LANES), BF16),
            pltpu.VMEM((2, ring, count, half), BF16),
            pltpu.VMEM((4, hops, count, half + LANES), BF16),
            pltpu.VMEM((4, hops, count, half + LANES), BF16),
            pltpu.VMEM((4, hops, count, half + LANES), BF16),
            pltpu.VMEM((4, hops, count, half + LANES), BF16),
            pltpu.VMEM((LANES, LANES), F32),
            dma((3,)),
            dma((4,)),
            dma((4, 2 * ring + 1)),
            dma((4, 2 * ring + 1)),
            dma((4, ring + 1)),
            dma((4, ring + 1)),
        ],
        compiler_params=pltpu.CompilerParams(
            collective_id=0, has_side_effects=True, vmem_limit_bytes=60 * 1024 * 1024
        ),
        cost_estimate=pl.CostEstimate(
            flops=12 * rows * width * hid,
            bytes_accessed=6 * width * hid + 4 * rows * (width + hid),
            transcendentals=rows * hid,
        ),
    )(quant, scales, routes.T, gates.T, cotangent, w_gate, w_up, w_down)
    x_all = x_all.reshape(rows, width)
    step = 512
    grad_up, grad_down = pl.pallas_call(
        weight_grads,
        grid=(width // step,),
        out_shape=(sds((1, width, hid), BF16), sds((1, hid, width), BF16)),
        in_specs=[
            pl.BlockSpec((rows, step), lambda n: (0, n)),
            pl.BlockSpec((rows, hid), lambda n: (0, 0)),
            pl.BlockSpec((rows, hid), lambda n: (0, 0)),
            pl.BlockSpec((rows, step), lambda n: (0, n)),
        ],
        out_specs=(
            pl.BlockSpec((1, step, hid), lambda n: (0, n, 0)),
            pl.BlockSpec((1, hid, step), lambda n: (0, 0, n)),
        ),
        scratch_shapes=[pltpu.VMEM((hid, rows), BF16)],
        compiler_params=pltpu.CompilerParams(vmem_limit_bytes=32 * 1024 * 1024),
        cost_estimate=pl.CostEstimate(
            flops=4 * rows * width * hid,
            bytes_accessed=4 * width * hid + 4 * rows * (width + hid),
            transcendentals=0,
        ),
    )(x_all, up_grad, hidden, row_grad)
    return (
        mixed,
        grad_tokens,
        grad_gates.T,
        grad_up,
        grad_down,
    )


def solution(mesh):
    rows = P(("groups", "expert", "cuts"), None)
    in_specs = (rows,) * 5 + (
        P("expert", None, "cuts"),
        P("expert", None, "cuts"),
        P("expert", "cuts", None),
    )
    out_specs = (rows,) * 3 + (
        P(("groups", "expert"), None, "cuts"),
        P(("groups", "expert"), "cuts", None),
    )
    return jax.shard_map(local, mesh=mesh, in_specs=in_specs, out_specs=out_specs, check_vma=False)
```

```python
import functools

import jax
import jax.numpy as jnp
from jax import lax
from jax.experimental import pallas as pl
from jax.experimental.pallas import tpu as pltpu
from jax.sharding import PartitionSpec as P

MESH = pl.DeviceIdType.MESH
LANES = 128
NT = (((1,), (1,)), ((), ()))
TN = (((0,), (0,)), ((), ()))
F32 = jnp.float32
BF16 = jnp.bfloat16


def parts_of(value):
    high = value.astype(BF16)
    rest = value - high.astype(F32)
    middle = rest.astype(BF16)
    return high, middle, (rest - middle.astype(F32)).astype(BF16)


def kernel(
    experts, cuts, quant, scales, routes, gates, cot, wg_hbm, wu_hbm, wd_hbm,
    mixed, grad_tokens, grad_gates, x_out, up_out, hidden_out, row_out,
    xg, cg, wg, wu, wd, rg, hidden, gate_grad, up_grad, slope, act, weight, dot_acc,
    mix_part, dx_part, sib_mix, sib_dx, out_r, in_r, out_l, in_l,
    turn, x_turned, hidden_turned, w_sem, o_sem, gs_sem, gr_sem, rs_sem, rr_sem,
):
    devices = experts * cuts
    ring = devices // 2
    count, width = quant.shape
    rows = devices * count
    hid = wg.shape[1]
    tile = 256 if hid % 256 == 0 else 128
    col = 256
    half = width // 2

    expert = lax.axis_index("expert")
    me = expert * cuts + lax.axis_index("cuts")
    core = lax.rem(me, 2)
    chip = me // 2

    def chip_at(p):
        if cuts > 1:
            return p
        upper = p // (ring // 2)
        return upper * (2 * (ring - 1 - p) + 1) + (1 - upper) * 2 * p

    if cuts > 1:
        pos = chip
    else:
        y = lax.rem(chip, 2)
        z = chip // 2
        pos = z + y * (ring - 1 - 2 * z)

    def wrap(p):
        return lax.rem(p + 2 * ring, ring)

    def device(p, c):
        i = chip_at(p) * 2 + c
        return {"expert": i // cuts, "cuts": lax.rem(i, cuts)}

    right = device(wrap(pos + 1), core)
    left = device(wrap(pos - 1), core)
    sibling = device(pos, 1 - core)

    loads = [
        pltpu.make_async_copy(src.at[0], dst, w_sem.at[n])
        for n, (src, dst) in enumerate(((wg_hbm, wg), (wu_hbm, wu), (wd_hbm, wd)))
    ]
    for load in loads:
        load.start()

    own = core * ring + pos
    for b in range(scales.shape[1]):
        block = pl.ds(b * (width // scales.shape[1]), width // scales.shape[1])
        xg[own, :, block] = (
            quant[:, block].astype(F32) * scales[:, b : b + 1].astype(F32)
        ).astype(BF16)
    tops = routes.shape[0]
    lane = lax.broadcasted_iota(jnp.int32, (count, LANES), 1)
    sub = lax.broadcasted_iota(jnp.int32, (LANES, count), 0)
    pay_t = jnp.zeros((LANES, count), F32)
    for k in range(tops):
        pay_t += jnp.where(sub == routes[k : k + 1, :], gates[k : k + 1, :], 0.0)
    turn[...] = jnp.zeros_like(turn)
    turn[:, 0:count] = pay_t
    pay = turn[...].T[0:count, :]
    cg[own, :, 0:width] = cot[...]
    packed = jnp.zeros((count, LANES), F32)
    for n, part in enumerate(parts_of(pay)):
        part = part.astype(F32)
        shifted = part if n == 0 else pltpu.roll(part, n * experts, 1)
        packed += shifted
    cg[own, :, width : width + LANES] = packed.astype(BF16)

    barrier = pltpu.get_barrier_semaphore()
    for other in (left, right, sibling):
        pl.semaphore_signal(barrier, inc=1, device_id=other, device_id_type=MESH)
    pl.semaphore_wait(barrier, 3)

    sends = []
    hops = ring // 2
    shares = ((hops, ring - 1 - hops), (ring - 1 - hops, hops))

    def gather(job, buf, lo, wide, hops_r, hops_l):
        def move(p, c, n, to):
            ref = buf.at[c * ring + p, :, pl.ds(lo, wide)]
            return pltpu.make_async_remote_copy(
                src_ref=ref, dst_ref=ref, send_sem=gs_sem.at[job, n],
                recv_sem=gr_sem.at[job, n], device_id=to, device_id_type=MESH,
            )

        def go(p, n, to):
            copy = move(p, core, n, to)
            copy.start()
            sends.append(copy)

        def step(s):
            if s == 0:
                go(pos, 0, right)
                go(pos, hops, left)
                go(pos, 2 * hops, sibling)
                return
            if s <= hops_r:
                p = wrap(pos - s)
                move(p, core, s - 1, right).wait_recv()
                if s < hops_r:
                    go(p, s, right)
                go(p, 2 * hops + s, sibling)
            if s <= hops_l:
                p = wrap(pos + s)
                move(p, core, hops + s - 1, left).wait_recv()
                if s < hops_l:
                    go(p, hops + s, left)
                go(p, 3 * hops + s, sibling)

        def finish():
            move(pos, 1 - core, 2 * hops, sibling).wait_recv()
            for s in range(1, hops_r + 1):
                move(wrap(pos - s), 1 - core, 2 * hops + s, sibling).wait_recv()
            for s in range(1, hops_l + 1):
                move(wrap(pos + s), 1 - core, 3 * hops + s, sibling).wait_recv()

        return step, finish

    x_jobs = [gather(0, xg, 0, half, *shares[0]), gather(1, xg, half, half, *shares[1])]
    c_jobs = [
        gather(2, cg, 0, half, *shares[0]),
        gather(3, cg, half, half + LANES, *shares[1]),
    ]
    for s in range(hops + 1):
        for step, _ in x_jobs:
            step(s)
        if s < hops:
            for step, _ in c_jobs:
                step(s)
    for _, finish in x_jobs:
        finish()
    outs = []

    def store(n, src, dst):
        copy = pltpu.make_async_copy(src, dst, o_sem.at[n])
        copy.start()
        outs.append(copy)


    def up_tiles(first, last):
        @pl.loop(first, last)
        def _(n):
            cols = pl.ds(pl.multiple_of(n * tile, tile), tile)
            x = xg[...].reshape(rows, width)
            gate = jnp.dot(x, wg[:, cols], preferred_element_type=F32)
            up = jnp.dot(x, wu[:, cols], preferred_element_type=F32)
            sig = jax.nn.sigmoid(gate)
            active = gate * sig
            act[:, cols] = active
            slope[:, cols] = up * sig * (1.0 + gate * (1.0 - sig))
            hidden[:, cols] = (active * up).astype(BF16)

    loads[0].wait()
    loads[1].wait()
    tiles = hid // tile
    up_tiles(0, 1)
    for step, _ in c_jobs:
        step(hops)
    up_tiles(1, tiles)
    for _, finish in c_jobs:
        finish()

    row_lane = lax.broadcasted_iota(jnp.int32, (rows, LANES), 1)
    mine = (row_lane == expert) | (row_lane == expert + experts)
    mine = mine | (row_lane == expert + 2 * experts)
    got = cg[:, :, width : width + LANES].reshape(rows, LANES).astype(F32)
    weight[...] = jnp.broadcast_to(
        jnp.sum(jnp.where(mine, got, 0.0), 1, keepdims=True), (rows, LANES)
    )
    loads[2].wait()
    dot_acc[...] = jnp.zeros_like(dot_acc)

    def out_tiles(first, last):
        @pl.loop(first, last)
        def _(n):
            cols = pl.ds(pl.multiple_of(n * col, col), col)
            out = jnp.dot(hidden[...], wd[:, cols], preferred_element_type=F32)
            c = cg[:, :, cols].reshape(rows, col).astype(F32)
            w = weight[:, 0:1]
            dot_acc[...] += c * out
            rg[:, cols] = (w * c).astype(BF16)
            mix_part[:, :, cols] = (w * out).astype(BF16).reshape(devices, count, col)

    def reduce(job, buf, sib, lo, wide, hops_r, hops_l):
        cols = pl.ds(lo, wide)
        narrow = pl.ds(0, wide)

        def copy(src, dst, n, to):
            return pltpu.make_async_remote_copy(
                src_ref=src, dst_ref=dst, send_sem=rs_sem.at[job, n],
                recv_sem=rr_sem.at[job, n], device_id=to, device_id_type=MESH,
            )

        def swap_cores():
            c = copy(
                buf.at[pl.ds((1 - core) * ring, ring), :, cols], sib, 2 * hops, sibling
            )
            c.start()
            sends.append(c)
            return c

        state = {"next": 0}

        def begin():
            state["sib"] = swap_cores()

        def base(p):
            return buf[core * ring + p, :, cols].astype(F32) + sib[p].astype(F32)

        def ring_copy(s, go_right):
            if go_right:
                return copy(out_r.at[job, s, :, narrow], in_r.at[job, s, :, narrow], s, right)
            return copy(out_l.at[job, s, :, narrow], in_l.at[job, s, :, narrow], hops + s, left)

        def hop():
            s = state["next"]
            if s == hops:
                return
            state["next"] = s + 1
            if s == 0:
                state["sib"].wait_recv()
            for go_right, most, outb, inb in (
                (True, hops_r, out_r, in_r), (False, hops_l, out_l, in_l)
            ):
                if s >= most:
                    continue
                p = wrap(pos + most - s) if go_right else wrap(pos - most + s)
                total = base(p)
                if s > 0:
                    ring_copy(s - 1, go_right).wait_recv()
                    total += inb[job, s - 1, :, narrow].astype(F32)
                outb[job, s, :, narrow] = total.astype(BF16)
                c = ring_copy(s, go_right)
                c.start()
                sends.append(c)

        def last():
            ring_copy(hops_r - 1, True).wait_recv()
            ring_copy(hops_l - 1, False).wait_recv()
            return (
                base(pos)
                + in_r[job, hops_r - 1, :, narrow].astype(F32)
                + in_l[job, hops_l - 1, :, narrow].astype(F32)
            )

        return begin, hop, last

    mix0 = reduce(0, mix_part, sib_mix.at[0, :, :, pl.ds(0, half)], 0, half, *shares[0])
    mix1 = reduce(1, mix_part, sib_mix.at[1], half, half + LANES, *shares[1])
    dx0 = reduce(2, dx_part, sib_dx.at[0], 0, half, *shares[0])
    dx1 = reduce(3, dx_part, sib_dx.at[1], half, half, *shares[1])

    per_half = half // col
    out_tiles(0, per_half)
    mix0[0]()
    out_tiles(per_half, 2 * per_half)
    store(2, rg, row_out)
    dots = jnp.sum(dot_acc[...], 1, keepdims=True)
    extra = jnp.zeros((rows, LANES), F32)
    for n, part in enumerate(parts_of(dots)):
        extra += jnp.where(row_lane == me + n * devices, part.astype(F32), 0.0)
    mix_part[:, :, width : width + LANES] = extra.astype(BF16).reshape(devices, count, LANES)
    mix1[0]()
    mix0[1]()

    def hidden_tiles(first, last):
        @pl.loop(first, last)
        def _(n):
            cols = pl.ds(pl.multiple_of(n * tile, tile), tile)
            grad = lax.dot_general(rg[...], wd[cols, :], NT, preferred_element_type=F32)
            gate_grad[:, cols] = (grad * slope[:, cols]).astype(BF16)
            up_grad[:, cols] = (grad * act[:, cols]).astype(BF16)

    def dx_tiles(first, last):
        @pl.loop(first, last)
        def _(n):
            cols = pl.ds(pl.multiple_of(n * col, col), col)
            dx = lax.dot_general(gate_grad[...], wg[cols, :], NT, preferred_element_type=F32)
            dx += lax.dot_general(up_grad[...], wu[cols, :], NT, preferred_element_type=F32)
            dx_part[:, :, cols] = dx.astype(BF16).reshape(devices, count, col)

    hidden_tiles(0, 2)
    mix1[1]()
    mix0[1]()
    hidden_tiles(2, 4)
    mix1[1]()
    mix0[1]()
    hidden_tiles(4, tiles)
    store(3, up_grad, up_out)
    dx_tiles(0, 2)
    mix1[1]()
    mix0[1]()
    dx_tiles(2, 5)
    mix1[1]()
    dx_tiles(5, per_half)
    dx0[0]()
    dx_tiles(per_half, per_half + 2)
    dx0[1]()
    dx_tiles(per_half + 2, per_half + 5)
    dx0[1]()
    dx_tiles(per_half + 5, 2 * per_half)
    dx1[0]()
    dx0[1]()
    def turn_rows(first, last):
        @pl.loop(first, last)
        def _(n):
            cols = pl.ds(pl.multiple_of(n * col, col), col)
            x_turned[cols, :] = xg[:, :, cols].reshape(rows, col).T

    def turn_hidden(first, last):
        @pl.loop(first, last)
        def _(n):
            cols = pl.ds(pl.multiple_of(n * tile, tile), tile)
            hidden_turned[cols, :] = hidden[:, cols].T

    turn_hidden(0, tiles)
    store(1, hidden_turned, hidden_out)
    for s in range(hops):
        for job in (mix0, mix1, dx1, dx0):
            job[1]()
        if s < 2:
            turn_rows(s * per_half, (s + 1) * per_half)
            if s == 1:
                store(0, x_turned, x_out)

    mixed[:, 0:half] = mix0[2]().astype(BF16)
    rest = mix1[2]()
    mixed[:, half:width] = rest[:, 0:half].astype(BF16)
    sums = rest[:, half : half + LANES]
    turn[0:count, :] = sums
    sums_t = turn[...].T[:, 0:count]
    for k in range(tops):
        base_lane = routes[k : k + 1, :] * cuts
        picked = sub < 0
        for n in range(3):
            for c in range(cuts):
                picked = picked | (sub == base_lane + (c + n * devices))
        grad_gates[k : k + 1, :] = jnp.sum(jnp.where(picked, sums_t, 0.0), 0, keepdims=True)
    grad_tokens[:, 0:half] = dx0[2]().astype(BF16)
    grad_tokens[:, half:width] = dx1[2]().astype(BF16)

    for copy in sends:
        copy.wait_send()
    for copy in outs:
        copy.wait()


def weight_grads(
    x_turned, up_grad, hidden_turned, row_grad, mixed, grad_tokens, grad_gates,
    grad_up, grad_down, mixed_out, tokens_out, gates_out,
):
    @pl.when(pl.program_id(0) == 0)
    def _():
        mixed_out[...] = mixed[...]
        tokens_out[...] = grad_tokens[...]
        gates_out[...] = grad_gates[...]

    grad_up[0] = jnp.dot(
        x_turned[...], up_grad[...], preferred_element_type=F32
    ).astype(BF16)
    grad_down[0] = jnp.dot(
        hidden_turned[...], row_grad[...], preferred_element_type=F32
    ).astype(BF16)


def local(quant, scales, routes, gates, cotangent, w_gate, w_up, w_down):
    cuts = lax.axis_size("cuts")
    experts = lax.axis_size("expert")
    devices = experts * cuts
    ring = devices // 2
    hops = ring // 2
    count, width = quant.shape
    hid = w_gate.shape[2]
    rows = devices * count
    half = width // 2
    vmem = pl.BlockSpec(memory_space=pltpu.VMEM)
    hbm = pl.BlockSpec(memory_space=pl.ANY)
    sds = jax.ShapeDtypeStruct
    dma = pltpu.SemaphoreType.DMA
    mixed, grad_tokens, grad_gates, x_all, up_grad, hidden, row_grad = pl.pallas_call(
        functools.partial(kernel, experts, cuts),
        out_shape=(
            sds((count, width), BF16),
            sds((count, width), BF16),
            sds(gates.shape[::-1], F32),
            sds((width, rows), BF16),
            sds((rows, hid), BF16),
            sds((hid, rows), BF16),
            sds((rows, width), BF16),
        ),
        in_specs=[vmem] * 5 + [hbm] * 3,
        out_specs=(vmem,) * 3 + (hbm,) * 4,
        scratch_shapes=[
            pltpu.VMEM((devices, count, width), BF16),
            pltpu.VMEM((devices, count, width + LANES), BF16),
            pltpu.VMEM((width, hid), BF16),
            pltpu.VMEM((width, hid), BF16),
            pltpu.VMEM((hid, width), BF16),
            pltpu.VMEM((rows, width), BF16),
            pltpu.VMEM((rows, hid), BF16),
            pltpu.VMEM((rows, hid), BF16),
            pltpu.VMEM((rows, hid), BF16),
            pltpu.VMEM((rows, hid), F32),
            pltpu.VMEM((rows, hid), F32),
            pltpu.VMEM((rows, LANES), F32),
            pltpu.VMEM((rows, 256), F32),
            pltpu.VMEM((devices, count, width + LANES), BF16),
            pltpu.VMEM((devices, count, width), BF16),
            pltpu.VMEM((2, ring, count, half + LANES), BF16),
            pltpu.VMEM((2, ring, count, half), BF16),
            pltpu.VMEM((4, hops, count, half + LANES), BF16),
            pltpu.VMEM((4, hops, count, half + LANES), BF16),
            pltpu.VMEM((4, hops, count, half + LANES), BF16),
            pltpu.VMEM((4, hops, count, half + LANES), BF16),
            pltpu.VMEM((LANES, LANES), F32),
            pltpu.VMEM((width, rows), BF16),
            pltpu.VMEM((hid, rows), BF16),
            dma((3,)),
            dma((4,)),
            dma((4, 2 * ring + 1)),
            dma((4, 2 * ring + 1)),
            dma((4, ring + 1)),
            dma((4, ring + 1)),
        ],
        compiler_params=pltpu.CompilerParams(
            collective_id=0, has_side_effects=True, vmem_limit_bytes=60 * 1024 * 1024
        ),
        cost_estimate=pl.CostEstimate(
            flops=12 * rows * width * hid,
            bytes_accessed=6 * width * hid + 4 * rows * (width + hid),
            transcendentals=rows * hid,
        ),
    )(quant, scales, routes.T, gates.T, cotangent, w_gate, w_up, w_down)
    step = 512
    small = [
        pl.BlockSpec(array.shape, lambda n: (0, 0))
        for array in (mixed, grad_tokens, grad_gates)
    ]
    grad_up, grad_down, mixed, grad_tokens, grad_gates = pl.pallas_call(
        weight_grads,
        grid=(width // step,),
        out_shape=(
            sds((1, width, hid), BF16),
            sds((1, hid, width), BF16),
            sds(mixed.shape, BF16),
            sds(grad_tokens.shape, BF16),
            sds(grad_gates.shape, F32),
        ),
        in_specs=[
            pl.BlockSpec((step, rows), lambda n: (n, 0)),
            pl.BlockSpec((rows, hid), lambda n: (0, 0)),
            pl.BlockSpec((hid, rows), lambda n: (0, 0)),
            pl.BlockSpec((rows, step), lambda n: (0, n)),
            *small,
        ],
        out_specs=(
            pl.BlockSpec((1, step, hid), lambda n: (0, n, 0)),
            pl.BlockSpec((1, hid, step), lambda n: (0, 0, n)),
            *small,
        ),
        compiler_params=pltpu.CompilerParams(vmem_limit_bytes=60 * 1024 * 1024),
        cost_estimate=pl.CostEstimate(
            flops=4 * rows * width * hid,
            bytes_accessed=4 * width * hid + 4 * rows * (width + hid),
            transcendentals=0,
        ),
    )(x_all, up_grad, hidden, row_grad, mixed, grad_tokens, grad_gates)
    return (
        mixed,
        grad_tokens,
        grad_gates.T,
        grad_up,
        grad_down,
    )


def solution(mesh):
    rows = P(("groups", "expert", "cuts"), None)
    in_specs = (rows,) * 5 + (
        P("expert", None, "cuts"),
        P("expert", None, "cuts"),
        P("expert", "cuts", None),
    )
    out_specs = (rows,) * 3 + (
        P(("groups", "expert"), None, "cuts"),
        P(("groups", "expert"), "cuts", None),
    )
    return jax.shard_map(local, mesh=mesh, in_specs=in_specs, out_specs=out_specs, check_vma=False)
```
